32 devices in a mesh: groups: 2 (over x), tensor: 8 (over z, y), replica: 2 (over core).
Axes of the slice: x: 2, y: 2, z: 4, core: 2. Of those that a mesh axis runs over, the one named last changes fastest.
Arguments:
- query: bfloat16 [32, 8192], P(('groups', 'replica'), 'tensor'), parts along dimension 0
- cached_key_rows: bfloat16 [32, 1024, 1024], P(('groups', 'replica', 'tensor')), parts along dimension 0
- cached_value_rows: bfloat16 [32, 1024, 1024], P(('groups', 'replica', 'tensor')), parts along dimension 0, may hold values from -6 to 6
- lengths: int32 [32], P(('groups', 'replica', 'tensor')), parts along dimension 0, may hold values from 64 to 1024, as said below
- request_adapter_index: int32 [32], P('groups'), parts along dimension 0, may hold values from 0 to 63
- output_projection_weight: bfloat16 [8192, 8192], P('tensor'), may hold values from -0.0625 to 0.0625
- adapter_down_weight: bfloat16 [128, 64, 8192], P(('groups', 'replica'), None, 'tensor'), parts along dimension 0, may hold values from -0.0625 to 0.0625
- adapter_up_weight: bfloat16 [128, 64, 8192], P(('groups', 'replica'), None, 'tensor'), parts along dimension 0, may hold values from -0.75 to 0.75
Outputs:
- attention_out: bfloat16 [32, 8192], P(('groups', 'replica'), 'tensor'), parts along dimension 0
The draws below stay inside these ranges and needn't reach their ends.
There are 2 independent parts, one for each index of `groups`. The reference program is written for one: setup_inputs(seed, part) draws one part's arguments, and reference() takes and returns one part's arrays. A program takes and returns all parts, laid end to end along the dimension named above; an argument that names none is the same for every part. Nothing has to cross between parts.
Inputs may be any that keep to these rules, and one draw needn't show every extreme that they name: `lengths`: one request has 1024 live slots and one has 64.
All inputs are finite; a program needn't handle non-finite values.
Results may differ from the reference program's by a relative error of at most 0.0061.
Values may be sent and summed in bfloat16 or wider, within the bound.
A program may use at most 128 MiB of HBM per device.

```python
import math
import jax
import jax.numpy as jnp
import numpy as np
from jax import lax

MODEL_WIDTH = 8192
HEADS = 64
KV_HEADS = 8
HEAD_DIM = 128
ADAPTER_RANK = 64
CACHE = 1024
GROUP = 8
QUERY_WIDTH = 8192
KVW = 1024
REQUESTS = 16
ADAPTER_TOTAL = 64


def shared_keys(key, tweak):
    base_keys = jax.random.normal(key, (REQUESTS, CACHE, KV_HEADS * HEAD_DIM), jnp.float32)
    request = jnp.arange(REQUESTS)
    chosen = (request % 8 == 0).astype(jnp.float32) * tweak
    strength = 10.0 + 2.0 * (request // 8 % 11).astype(jnp.float32)
    factor = 1.0 + 2.0 / (strength * math.sqrt(HEAD_DIM))
    second_row = base_keys[:, 0] * factor[:, None]
    second_row = jnp.where(chosen[:, None] > 0, second_row, base_keys[:, 1])
    return (base_keys.at[:, 1].set(second_row), strength, chosen)


def draw_cached_key_rows(key, part):
    tweak = 0.0
    keys_all, strength, chosen = shared_keys(key, tweak)
    return keys_all.astype(jnp.bfloat16)


def draw_query(key, part):
    tweak = 0.0
    keys_all, strength, chosen = shared_keys(key, tweak)
    key = jax.random.fold_in(key, 5)
    noise = jax.random.normal(key, (REQUESTS, KV_HEADS, GROUP, HEAD_DIM), jnp.float32)
    target = keys_all[:, 0].reshape(REQUESTS, KV_HEADS, 1, HEAD_DIM) * strength[:, None, None, None]
    leading = jnp.arange(GROUP) == 0
    picked = (chosen[:, None, None, None] > 0) & leading[None, None, :, None]
    mixed = jnp.where(picked, target, noise)
    return mixed.reshape(REQUESTS, HEADS * HEAD_DIM).astype(jnp.bfloat16)


def draw_lengths(key, part):
    key = jax.random.fold_in(key, 7)
    values = jax.random.randint(key, (REQUESTS,), CACHE // 16, CACHE + 1, jnp.int32)
    values = values.at[0].set(CACHE)
    return values.at[1].set(CACHE // 16)


def touch_ends(result, own_key, smallest, top_value):
    dims = result.shape
    index_at = [jax.random.randint(jax.random.fold_in(own_key, axis), (), 0, dims[axis]) for axis in range(len(dims))]
    result = result.at[tuple(index_at)].set(smallest)
    longest = dims.index(max(dims))
    index_at[longest] = (index_at[longest] + 1) % dims[longest]
    return result.at[tuple(index_at)].set(top_value)


def steps_of(key, shape, shards, smallest, high):
    gain, own = 1.0, jax.random.fold_in(key, 6)
    for axis_at, parts in shards:
        heights = jnp.exp(jax.random.uniform(jax.random.fold_in(own, axis_at), (parts,), jnp.float32, smallest / len(shards), high / len(shards)))
        gain = gain * jnp.repeat(heights, shape[axis_at] // parts).reshape([-1 if axis == axis_at else 1 for axis in range(len(shape))])
    return gain


def rank_bounds(number_of, slope):
    portions = [(1 << 20) // math.isqrt(rank ** slope) + 1 for rank in range(1, number_of + 1)]
    width = 1 + sum(portions) // (1 << 30)
    return np.cumsum(np.array([max(1, weight // width) for weight in portions]))


def skewed_ids(own_key, shape, count, slope):
    listing = rank_bounds(count, slope)
    pick = jax.random.randint(jax.random.fold_in(own_key, 1), shape, 0, int(listing[count - 1]))
    standing = jnp.searchsorted(jnp.asarray(listing, jnp.int32), pick, side="right")
    return jax.random.permutation(jax.random.fold_in(own_key, 2), count)[standing].astype(jnp.int32)


def bell_draw(own_key, dims, scale, reach, pieces=(), held_as=jnp.bfloat16):
    values = scale * jax.random.normal(own_key, dims, jnp.float32)
    if pieces:
        values = values * steps_of(own_key, dims, pieces, -0.22, 0.18)
    return jnp.clip(values, -reach, reach).astype(held_as)


def setup_inputs(seed: int = 0, part: int = 0) -> dict:
    key_of = jax.random.split(jax.random.key(seed), 9)
    own_keys = jax.random.split(jax.random.fold_in(key_of[8], part), 9)
    return {
        "query": draw_query(jax.random.fold_in(jax.random.fold_in(key_of[8], part), 71), part),
        "cached_key_rows": draw_cached_key_rows(jax.random.fold_in(jax.random.fold_in(key_of[8], part), 71), part),
        "cached_value_rows": bell_draw(own_keys[2], (REQUESTS, CACHE, KVW), 1.0, 6.0, ((0, 16),)),
        "lengths": draw_lengths(jax.random.fold_in(jax.random.fold_in(key_of[8], part), 71), part),
        "request_adapter_index": touch_ends(skewed_ids(own_keys[4], (REQUESTS,), ADAPTER_TOTAL, 2), jax.random.fold_in(own_keys[4], 3), 0, ADAPTER_TOTAL - 1).astype(jnp.int32),
        "output_projection_weight": bell_draw(key_of[5], (QUERY_WIDTH, MODEL_WIDTH), QUERY_WIDTH ** -0.5, 0.0625, ((0, 8),)),
        "adapter_down_weight": bell_draw(own_keys[6], (ADAPTER_TOTAL, ADAPTER_RANK, QUERY_WIDTH), QUERY_WIDTH ** -0.5, 0.0625, ((0, 2), (2, 8))),
        "adapter_up_weight": bell_draw(own_keys[7], (ADAPTER_TOTAL, ADAPTER_RANK, MODEL_WIDTH), ADAPTER_RANK ** -0.5, 0.75, ((0, 2), (2, 8))),
    }


def attend_one(operands):
    query_row, key_block, value_block, live_count = operands
    grouped = query_row.astype(jnp.float32).reshape(KV_HEADS, GROUP, HEAD_DIM)
    key_heads = key_block.astype(jnp.float32).reshape(CACHE, KV_HEADS, HEAD_DIM)
    value_heads = value_block.astype(jnp.float32).reshape(CACHE, KV_HEADS, HEAD_DIM)
    scores = jnp.einsum("kgd,ckd->kgc", grouped, key_heads) * (HEAD_DIM ** -0.5)
    live_mask = jnp.arange(CACHE) < live_count
    scores = jnp.where(live_mask, scores, -1e30)
    top_score = jnp.max(scores, axis=-1, keepdims=True)
    exp_terms = jnp.where(live_mask, jnp.exp(scores - top_score), 0.0)
    weights = (exp_terms / jnp.sum(exp_terms, axis=-1, keepdims=True)).astype(jnp.bfloat16)
    attended = jnp.einsum("kgc,ckd->kgd", weights.astype(jnp.float32), value_heads)
    return attended.reshape(QUERY_WIDTH).astype(jnp.bfloat16)


def reference(query, cached_key_rows, cached_value_rows, lengths, request_adapter_index, output_projection_weight, adapter_down_weight, adapter_up_weight):
    attended = lax.map(attend_one, (query, cached_key_rows, cached_value_rows, lengths))
    base_sum = jnp.dot(attended, output_projection_weight, preferred_element_type=jnp.float32)

    def adapt(operands):
        attended_row, identity_matrix = operands
        down_matrix_panel = lax.dynamic_index_in_dim(adapter_down_weight, identity_matrix, 0, keepdims=False)
        up_matrix_panel = lax.dynamic_index_in_dim(adapter_up_weight, identity_matrix, 0, keepdims=False)
        shrink = jnp.dot(down_matrix_panel, attended_row, preferred_element_type=jnp.float32).astype(jnp.bfloat16)
        return jnp.dot(shrink, up_matrix_panel, preferred_element_type=jnp.float32)

    delta = lax.map(adapt, (attended, request_adapter_index.astype(jnp.int32)))
    return (base_sum + delta).astype(jnp.bfloat16)
```

```python
import functools

import jax
import jax.numpy as jnp
from jax import lax
from jax.experimental import pallas as pl
from jax.experimental.pallas import tpu as pltpu
from jax.sharding import PartitionSpec as P

KV_HEADS = 8
HEAD_DIM = 128
GROUP = 8
MESH = pl.DeviceIdType.MESH
NT = (((1,), (1,)), ((), ()))
NN = (((1,), (0,)), ((), ()))


def kernel(
    T, RP, R, F, NB, RANK, AL, C,
    q_hbm, k_hbm, v_hbm, len_ref, idx_ref, w_hbm, dn_hbm, up_hbm, out_ref,
    q_v, k_v, v_v, w_v, dn_v, up_v,
    q_send, q_recv, a_send, a_recv, e_buf, p_send, p_recv, d_buf, d_recv,
    loc_sem, w_sem,
    qs_sem, qr_sem, as_sem, ar_sem, es_sem, er_sem, ps_sem, pr_sem, ds_sem, dr_sem,
):
    t = lax.axis_index("tensor")
    r = lax.axis_index("replica")
    N = T * RP
    me = r * T + t
    H = F // RP
    HL = F // HEAD_DIM
    FOLD = max(1, 16 // R)
    PACK = 256 // RANK

    q_cp = pltpu.make_async_copy(q_hbm, q_v, loc_sem.at[0])
    k_cp = pltpu.make_async_copy(k_hbm.at[0], k_v, loc_sem.at[1])
    v_cp = pltpu.make_async_copy(v_hbm.at[0], v_v, loc_sem.at[2])
    dn_cp = pltpu.make_async_copy(dn_hbm, dn_v, loc_sem.at[3])
    up_cp = pltpu.make_async_copy(up_hbm, up_v, loc_sem.at[4])

    def w_cp(tt):
        cols = pl.ds(pl.multiple_of(tt * F + r * H, 128), H)
        return pltpu.make_async_copy(w_hbm.at[:, cols], w_v.at[tt], w_sem.at[tt])

    q_cp.start()
    barrier = pltpu.get_barrier_semaphore()

    @pl.loop(1, N)
    def _(i):
        p = lax.rem(me + i, N)
        pl.semaphore_signal(
            barrier, inc=1,
            device_id={"tensor": lax.rem(p, T), "replica": lax.div(p, T)},
            device_id_type=MESH,
        )

    k_cp.start()
    v_cp.start()
    dn_cp.start()

    @pl.loop(1, T + 1)
    def _(i):
        w_cp(lax.rem(t + i, T)).start()

    up_cp.start()

    q_cp.wait()
    q_all = q_v[...].astype(jnp.float32)
    for h in range(HL):
        q_send[:, h, :] = q_all[:, h * HEAD_DIM:(h + 1) * HEAD_DIM]

    pl.semaphore_wait(barrier, N - 1)

    def q_rc(dst, src):
        return pltpu.make_async_remote_copy(
            src_ref=q_send.at[dst], dst_ref=q_recv.at[src],
            send_sem=qs_sem.at[dst], recv_sem=qr_sem.at[src],
            device_id={"tensor": dst}, device_id_type=MESH,
        )

    @pl.loop(1, T)
    def _(i):
        q_rc(lax.rem(t + i, T), t).start()

    q_recv[t] = q_send[t]
    k_cp.wait()

    @pl.loop(1, T)
    def _(i):
        q_rc(t, lax.rem(t + i, T)).wait_recv()

    n_per = T // KV_HEADS if T > KV_HEADS else 1
    live = len_ref[0]
    live_mask = lax.broadcasted_iota(jnp.int32, (2 * GROUP, C), 1) < live
    zero = jnp.zeros((GROUP, HEAD_DIM), jnp.float32)

    def heads_of(kv):
        if HL >= GROUP:
            per = HL // GROUP
            rows = q_recv[kv // per]
            return rows[(kv % per) * GROUP:(kv % per + 1) * GROUP]
        return jnp.concatenate([q_recv[kv * n_per + i] for i in range(n_per)], axis=0)

    weights = []
    for p in range(KV_HEADS // 2):
        pair = jnp.concatenate(
            [
                jnp.concatenate([heads_of(2 * p), zero], axis=1),
                jnp.concatenate([zero, heads_of(2 * p + 1)], axis=1),
            ],
            axis=0,
        ).astype(jnp.bfloat16)
        cols = slice(p * 2 * HEAD_DIM, (p + 1) * 2 * HEAD_DIM)
        s = lax.dot_general(pair, k_v[:, cols], NT, preferred_element_type=jnp.float32)
        s = jnp.where(live_mask, s * HEAD_DIM ** (-0.5), -1e30)
        top = jnp.max(s, axis=1, keepdims=True)
        e = jnp.where(live_mask, jnp.exp(s - top), 0.0)
        weights.append((e / jnp.sum(e, axis=1, keepdims=True)).astype(jnp.bfloat16))

    v_cp.wait()
    for p in range(KV_HEADS // 2):
        cols = slice(p * 2 * HEAD_DIM, (p + 1) * 2 * HEAD_DIM)
        o = lax.dot_general(weights[p], v_v[:, cols], NN, preferred_element_type=jnp.float32)
        o = o.astype(jnp.bfloat16).astype(jnp.float32)
        for half in range(2):
            kv = 2 * p + half
            rows = o[half * GROUP:(half + 1) * GROUP, half * HEAD_DIM:(half + 1) * HEAD_DIM]
            if HL >= GROUP:
                per = HL // GROUP
                a_send[kv // per, (kv % per) * GROUP:(kv % per + 1) * GROUP, :] = rows
            else:
                for i in range(n_per):
                    a_send[kv * n_per + i] = rows[i * HL:(i + 1) * HL]

    def a_rc(dst, src):
        return pltpu.make_async_remote_copy(
            src_ref=a_send.at[lax.rem(dst, T)], dst_ref=a_recv.at[src],
            send_sem=as_sem.at[dst], recv_sem=ar_sem.at[src],
            device_id={"tensor": lax.rem(dst, T), "replica": lax.div(dst, T)},
            device_id_type=MESH,
        )

    @pl.loop(1, N)
    def _(i):
        a_rc(lax.rem(me + i, N), me).start()

    a_recv[me] = a_send[t]
    dn_cp.wait()

    @pl.loop(1, N)
    def _(i):
        a_rc(me, lax.rem(me + i, N)).wait_recv()

    rows = jnp.concatenate(
        [a_recv[:, h, :] for h in range(HL)], axis=1
    ).astype(jnp.bfloat16)

    ids = [idx_ref[b] - r * AL for b in range(NB)]
    row2 = lax.broadcasted_iota(jnp.int32, (NB, 128), 0)
    here = jnp.zeros((NB, 128), jnp.int32)
    for b in range(NB):
        ok = jnp.where((ids[b] >= 0) & (ids[b] < AL), 1, 0)
        here = jnp.where(row2 == b, ok, here)
    local = [jnp.clip(i, 0, AL - 1) for i in ids]
    rowp = lax.broadcasted_iota(jnp.int32, (NB, 256), 0)
    slot = lax.broadcasted_iota(jnp.int32, (NB, 256), 1) // RANK
    part = jnp.zeros((NB, 256), jnp.float32)
    for j in range(NB // PACK):
        panels = jnp.concatenate([dn_v[local[j * PACK + b]] for b in range(PACK)], axis=0)
        o = lax.dot_general(rows, panels, NT, preferred_element_type=jnp.float32)
        part = jnp.where(rowp == j * PACK + slot, o, part)
    e_buf[t] = jnp.where(here > 0, part[:, :128] + part[:, 128:], 0.0)

    def e_rc(dst, src):
        return pltpu.make_async_remote_copy(
            src_ref=e_buf.at[src], dst_ref=e_buf.at[src],
            send_sem=es_sem.at[dst], recv_sem=er_sem.at[src],
            device_id={"tensor": dst}, device_id_type=MESH,
        )

    @pl.loop(1, T)
    def _(i):
        e_rc(lax.rem(t + i, T), t).start()

    def p_rc(dst, src):
        return pltpu.make_async_remote_copy(
            src_ref=p_send.at[dst], dst_ref=p_recv.at[src],
            send_sem=ps_sem.at[dst], recv_sem=pr_sem.at[src],
            device_id={"tensor": lax.rem(dst, T), "replica": lax.div(dst, T)},
            device_id_type=MESH,
        )

    def project(tt):
        w_cp(tt).wait()
        acc = lax.dot_general(rows, w_v[tt], NN, preferred_element_type=jnp.float32)
        for rr in range(RP):
            block = acc[rr * R:(rr + 1) * R]
            if FOLD > 1:
                wide = H // FOLD
                block = jnp.concatenate(
                    [block[:, f * wide:(f + 1) * wide] for f in range(FOLD)], axis=0
                )
            p_send[rr * T + tt] = block.astype(jnp.bfloat16)

    @pl.loop(1, T)
    def _(i):
        tt = lax.rem(t + i, T)
        project(tt)
        for rr in range(RP):
            p_rc(rr * T + tt, me).start()

    project(t)
    other = (1 - r) * T + t
    p_rc(other, me).start()
    p_recv[me] = p_send[me]

    up_cp.wait()

    @pl.loop(1, T)
    def _(i):
        e_rc(t, lax.rem(t + i, T)).wait_recv()

    total = e_buf[0]
    for i in range(1, T):
        total = total + e_buf[i]
    total = total.astype(jnp.bfloat16).astype(jnp.float32)
    total = jnp.concatenate([total, total], axis=1)
    delta = jnp.zeros((NB, F), jnp.float32)
    for j in range(NB // PACK):
        panels = jnp.concatenate([up_v[local[j * PACK + b]] for b in range(PACK)], axis=0)
        lhs = jnp.where(rowp == j * PACK + slot, total, 0.0).astype(jnp.bfloat16)
        delta = delta + lax.dot_general(lhs, panels, NN, preferred_element_type=jnp.float32)
    for rr in range(RP):
        d_buf[rr] = delta[rr * R:(rr + 1) * R]
    d_rc = pltpu.make_async_remote_copy(
        src_ref=d_buf.at[1 - r], dst_ref=d_recv,
        send_sem=ds_sem.at[0], recv_sem=dr_sem.at[0],
        device_id={"replica": 1 - r}, device_id_type=MESH,
    )
    d_rc.start()

    @pl.loop(1, N)
    def _(i):
        p_rc(me, lax.rem(me + i, N)).wait_recv()

    d_rc.wait_recv()
    for rr in range(RP):
        base = p_recv[rr * T].astype(jnp.float32)
        for i in range(1, T):
            base = base + p_recv[rr * T + i].astype(jnp.float32)
        if FOLD > 1:
            base = jnp.concatenate([base[f * R:(f + 1) * R] for f in range(FOLD)], axis=1)
        cols = slice(rr * H, (rr + 1) * H)
        add = d_buf[r, :, cols] + d_recv[:, cols]
        out_ref[:, cols] = (base + add).astype(jnp.bfloat16)

    @pl.loop(1, T)
    def _(i):
        dst = lax.rem(t + i, T)
        q_rc(dst, t).wait_send()
        e_rc(dst, t).wait_send()

    @pl.loop(1, N)
    def _(i):
        dst = lax.rem(me + i, N)
        a_rc(dst, me).wait_send()
        p_rc(dst, me).wait_send()

    d_rc.wait_send()


def solution(mesh):
    T = mesh.shape["tensor"]
    RP = mesh.shape["replica"]

    def local(query, keys, values, lengths, index, w, dn, up):
        R, F = query.shape
        NB = index.shape[0]
        AL, RANK, _ = dn.shape
        C = keys.shape[1]
        N = T * RP
        H = F // RP
        HL = F // HEAD_DIM
        FOLD = max(1, 16 // R)
        f32, b16 = jnp.float32, jnp.bfloat16
        dma = pltpu.SemaphoreType.DMA
        anyspec = pl.BlockSpec(memory_space=pl.ANY)
        smem = pl.BlockSpec(memory_space=pltpu.SMEM)
        return pl.pallas_call(
            functools.partial(kernel, T, RP, R, F, NB, RANK, AL, C),
            out_shape=jax.ShapeDtypeStruct((R, F), b16),
            in_specs=[anyspec, anyspec, anyspec, smem, smem, anyspec, anyspec, anyspec],
            out_specs=pl.BlockSpec(memory_space=pltpu.VMEM),
            scratch_shapes=[
                pltpu.VMEM((R, F), b16),
                pltpu.VMEM(keys.shape[1:], b16),
                pltpu.VMEM(values.shape[1:], b16),
                pltpu.VMEM((T, F, H), b16),
                pltpu.VMEM(dn.shape, b16),
                pltpu.VMEM(up.shape, b16),
                pltpu.VMEM((T, HL, HEAD_DIM), f32),
                pltpu.VMEM((T, HL, HEAD_DIM), f32),
                pltpu.VMEM((T, HL, HEAD_DIM), f32),
                pltpu.VMEM((N, HL, HEAD_DIM), f32),
                pltpu.VMEM((T, NB, 128), f32),
                pltpu.VMEM((N, R * FOLD, H // FOLD), b16),
                pltpu.VMEM((N, R * FOLD, H // FOLD), b16),
                pltpu.VMEM((RP, R, F), f32),
                pltpu.VMEM((R, F), f32),
                dma((5,)),
                dma((T,)),
                dma((T,)), dma((T,)),
                dma((N,)), dma((N,)),
                dma((T,)), dma((T,)),
                dma((N,)), dma((N,)),
                dma((1,)), dma((1,)),
            ],
            compiler_params=pltpu.CompilerParams(
                collective_id=0, has_side_effects=True,
                vmem_limit_bytes=48 * 1024 * 1024,
            ),
        )(query, keys, values, lengths, index, w, dn, up)

    return jax.shard_map(
        local,
        mesh=mesh,
        in_specs=(
            P(("groups", "replica"), "tensor"),
            P(("groups", "replica", "tensor"), None, None),
            P(("groups", "replica", "tensor"), None, None),
            P(("groups", "replica", "tensor")),
            P("groups"),
            P("tensor", None),
            P(("groups", "replica"), None, "tensor"),
            P(("groups", "replica"), None, "tensor"),
        ),
        out_specs=P(("groups", "replica"), "tensor"),
        check_vma=False,
    )
```

```python
import functools

import jax
import jax.numpy as jnp
from jax import lax
from jax.experimental import pallas as pl
from jax.experimental.pallas import tpu as pltpu
from jax.sharding import PartitionSpec as P

KV_HEADS = 8
HEAD_DIM = 128
GROUP = 8
MESH = pl.DeviceIdType.MESH
NT = (((1,), (1,)), ((), ()))
NN = (((1,), (0,)), ((), ()))


def kernel(
    T, RP, R, F, NB, RANK, AL, C,
    q_hbm, k_hbm, v_hbm, len_hbm, idx_hbm, w_hbm, dn_hbm, up_hbm, out_ref,
    len_ref, idx_ref, q_v, k_v, v_v, w_v, dn_v, up_v,
    q_send, q_recv, a_send, a_recv, e_buf, p_send, p_recv, d_buf, d_recv,
    loc_sem, w_sem,
    qs_sem, qr_sem, as_sem, ar_sem, es_sem, er_sem, ps_sem, pr_sem, ds_sem, dr_sem,
):
    t = lax.axis_index("tensor")
    r = lax.axis_index("replica")
    N = T * RP
    me = r * T + t
    H = F // RP
    HL = F // HEAD_DIM
    FOLD = max(1, 16 // R)
    PACK = 256 // RANK

    def wrap(x):
        return jnp.where(x >= T, x - T, x)

    q_cp = pltpu.make_async_copy(q_hbm, q_v, loc_sem.at[0])
    k_cp = pltpu.make_async_copy(k_hbm.at[0], k_v, loc_sem.at[1])
    v_cp = pltpu.make_async_copy(v_hbm.at[0], v_v, loc_sem.at[2])
    dn_cp = pltpu.make_async_copy(dn_hbm, dn_v, loc_sem.at[3])
    up_cp = pltpu.make_async_copy(up_hbm, up_v, loc_sem.at[4])

    def w_cp(tt):
        cols = pl.ds(pl.multiple_of(tt * F + r * H, 128), H)
        return pltpu.make_async_copy(w_hbm.at[:, cols], w_v.at[tt], w_sem.at[tt])

    len_cp = pltpu.make_async_copy(len_hbm, len_ref, loc_sem.at[5])
    idx_cp = pltpu.make_async_copy(idx_hbm, idx_ref, loc_sem.at[6])

    def many(buf, count, send, recv):
        part = buf.at[pl.ds(0, count)]
        return pltpu.make_async_remote_copy(
            src_ref=part, dst_ref=part, send_sem=send.at[0], recv_sem=recv.at[0],
            device_id={"replica": 1 - r}, device_id_type=MESH,
        )

    q_all_rc = many(q_recv, T - 1, qs_sem, qr_sem)
    a_all_rc = many(a_recv, N - 1, as_sem, ar_sem)
    e_all_rc = many(e_buf, T - 1, es_sem, er_sem)
    p_all_rc = many(p_recv, N - 1, ps_sem, pr_sem)

    q_cp.start()
    len_cp.start()
    idx_cp.start()
    barrier = pltpu.get_barrier_semaphore()

    def greet(rr, dst):
        pl.semaphore_signal(
            barrier, inc=1, device_id={"tensor": dst, "replica": rr}, device_id_type=MESH
        )

    @pl.loop(1, T)
    def _(i):
        for rr in range(RP):
            greet(rr, wrap(t + i))

    greet(1 - r, t)

    k_cp.start()
    v_cp.start()
    dn_cp.start()

    @pl.loop(1, T + 1)
    def _(i):
        w_cp(wrap(t + i)).start()

    up_cp.start()

    q_cp.wait()
    len_cp.wait()
    idx_cp.wait()
    q_all = q_v[...].astype(jnp.float32)
    for h in range(HL):
        q_send[:, h, :] = q_all[:, h * HEAD_DIM:(h + 1) * HEAD_DIM]

    pl.semaphore_wait(barrier, N - 1)

    def q_rc(dst, src):
        return pltpu.make_async_remote_copy(
            src_ref=q_send.at[dst], dst_ref=q_recv.at[src],
            send_sem=qs_sem.at[0], recv_sem=qr_sem.at[0],
            device_id={"tensor": dst}, device_id_type=MESH,
        )

    @pl.loop(1, T)
    def _(i):
        q_rc(wrap(t + i), t).start()

    q_recv[t] = q_send[t]
    k_cp.wait()

    q_all_rc.wait_recv()

    n_per = T // KV_HEADS if T > KV_HEADS else 1
    live = len_ref[0]
    live_mask = lax.broadcasted_iota(jnp.int32, (2 * GROUP, C), 1) < live
    zero = jnp.zeros((GROUP, HEAD_DIM), jnp.float32)

    def heads_of(kv):
        if HL >= GROUP:
            per = HL // GROUP
            rows = q_recv[kv // per]
            return rows[(kv % per) * GROUP:(kv % per + 1) * GROUP]
        return jnp.concatenate([q_recv[kv * n_per + i] for i in range(n_per)], axis=0)

    weights = []
    for p in range(KV_HEADS // 2):
        pair = jnp.concatenate(
            [
                jnp.concatenate([heads_of(2 * p), zero], axis=1),
                jnp.concatenate([zero, heads_of(2 * p + 1)], axis=1),
            ],
            axis=0,
        ).astype(jnp.bfloat16)
        cols = slice(p * 2 * HEAD_DIM, (p + 1) * 2 * HEAD_DIM)
        s = lax.dot_general(pair, k_v[:, cols], NT, preferred_element_type=jnp.float32)
        s = jnp.where(live_mask, s * HEAD_DIM ** (-0.5), -1e30)
        top = jnp.max(s, axis=1, keepdims=True)
        e = jnp.where(live_mask, jnp.exp(s - top), 0.0)
        weights.append((e / jnp.sum(e, axis=1, keepdims=True)).astype(jnp.bfloat16))

    v_cp.wait()
    for p in range(KV_HEADS // 2):
        cols = slice(p * 2 * HEAD_DIM, (p + 1) * 2 * HEAD_DIM)
        o = lax.dot_general(weights[p], v_v[:, cols], NN, preferred_element_type=jnp.float32)
        o = o.astype(jnp.bfloat16).astype(jnp.float32)
        for half in range(2):
            kv = 2 * p + half
            rows = o[half * GROUP:(half + 1) * GROUP, half * HEAD_DIM:(half + 1) * HEAD_DIM]
            if HL >= GROUP:
                per = HL // GROUP
                a_send[kv // per, (kv % per) * GROUP:(kv % per + 1) * GROUP, :] = rows
            else:
                for i in range(n_per):
                    a_send[kv * n_per + i] = rows[i * HL:(i + 1) * HL]

    def a_rc(rr, dst, src):
        return pltpu.make_async_remote_copy(
            src_ref=a_send.at[dst], dst_ref=a_recv.at[src],
            send_sem=as_sem.at[0], recv_sem=ar_sem.at[0],
            device_id={"tensor": dst, "replica": rr}, device_id_type=MESH,
        )

    a_rc(1 - r, t, me).start()

    @pl.loop(1, T)
    def _(i):
        dst = wrap(t + T - i)
        for rr in range(RP):
            a_rc(rr, dst, me).start()

    a_recv[me] = a_send[t]
    dn_cp.wait()

    a_all_rc.wait_recv()

    rows = jnp.concatenate(
        [a_recv[:, h, :] for h in range(HL)], axis=1
    ).astype(jnp.bfloat16)

    ids = [idx_ref[b] - r * AL for b in range(NB)]
    row2 = lax.broadcasted_iota(jnp.int32, (NB, 128), 0)
    here = jnp.zeros((NB, 128), jnp.int32)
    for b in range(NB):
        ok = jnp.where((ids[b] >= 0) & (ids[b] < AL), 1, 0)
        here = jnp.where(row2 == b, ok, here)
    local = [jnp.clip(i, 0, AL - 1) for i in ids]
    rowp = lax.broadcasted_iota(jnp.int32, (NB, 256), 0)
    slot = lax.broadcasted_iota(jnp.int32, (NB, 256), 1) // RANK
    part = jnp.zeros((NB, 256), jnp.float32)
    for j in range(NB // PACK):
        panels = jnp.concatenate([dn_v[local[j * PACK + b]] for b in range(PACK)], axis=0)
        o = lax.dot_general(rows, panels, NT, preferred_element_type=jnp.float32)
        part = jnp.where(rowp == j * PACK + slot, o, part)
    e_buf[t] = jnp.where(here > 0, part[:, :128] + part[:, 128:], 0.0)

    def e_rc(dst, src):
        return pltpu.make_async_remote_copy(
            src_ref=e_buf.at[src], dst_ref=e_buf.at[src],
            send_sem=es_sem.at[0], recv_sem=er_sem.at[0],
            device_id={"tensor": dst}, device_id_type=MESH,
        )

    @pl.loop(1, T)
    def _(i):
        e_rc(wrap(t + i), t).start()

    def p_rc(rr, dst, src):
        return pltpu.make_async_remote_copy(
            src_ref=p_send.at[rr * T + dst], dst_ref=p_recv.at[src],
            send_sem=ps_sem.at[0], recv_sem=pr_sem.at[0],
            device_id={"tensor": dst, "replica": rr}, device_id_type=MESH,
        )

    def project(tt):
        w_cp(tt).wait()
        acc = lax.dot_general(rows, w_v[tt], NN, preferred_element_type=jnp.float32)
        for rr in range(RP):
            block = acc[rr * R:(rr + 1) * R]
            if FOLD > 1:
                wide = H // FOLD
                block = jnp.concatenate(
                    [block[:, f * wide:(f + 1) * wide] for f in range(FOLD)], axis=0
                )
            p_send[rr * T + tt] = block.astype(jnp.bfloat16)

    @pl.loop(1, T)
    def _(i):
        tt = wrap(t + i)
        project(tt)
        for rr in range(RP):
            p_rc(rr, tt, me).start()

    project(t)
    p_rc(1 - r, t, me).start()
    p_recv[me] = p_send[me]

    up_cp.wait()

    e_all_rc.wait_recv()

    total = e_buf[0]
    for i in range(1, T):
        total = total + e_buf[i]
    total = total.astype(jnp.bfloat16).astype(jnp.float32)
    total = jnp.concatenate([total, total], axis=1)
    delta = jnp.zeros((NB, F), jnp.float32)
    for j in range(NB // PACK):
        panels = jnp.concatenate([up_v[local[j * PACK + b]] for b in range(PACK)], axis=0)
        lhs = jnp.where(rowp == j * PACK + slot, total, 0.0).astype(jnp.bfloat16)
        delta = delta + lax.dot_general(lhs, panels, NN, preferred_element_type=jnp.float32)
    for rr in range(RP):
        d_buf[rr] = delta[rr * R:(rr + 1) * R]
    d_rc = pltpu.make_async_remote_copy(
        src_ref=d_buf.at[1 - r], dst_ref=d_recv,
        send_sem=ds_sem.at[0], recv_sem=dr_sem.at[0],
        device_id={"replica": 1 - r}, device_id_type=MESH,
    )
    d_rc.start()

    q_all_rc.wait_send()
    e_all_rc.wait_send()
    a_all_rc.wait_send()

    p_all_rc.wait_recv()

    d_rc.wait_recv()
    for rr in range(RP):
        base = p_recv[rr * T].astype(jnp.float32)
        for i in range(1, T):
            base = base + p_recv[rr * T + i].astype(jnp.float32)
        if FOLD > 1:
            base = jnp.concatenate([base[f * R:(f + 1) * R] for f in range(FOLD)], axis=1)
        cols = slice(rr * H, (rr + 1) * H)
        add = d_buf[r, :, cols] + d_recv[:, cols]
        out_ref[:, cols] = (base + add).astype(jnp.bfloat16)

    p_all_rc.wait_send()

    d_rc.wait_send()


def solution(mesh):
    T = mesh.shape["tensor"]
    RP = mesh.shape["replica"]

    def local(query, keys, values, lengths, index, w, dn, up):
        R, F = query.shape
        NB = index.shape[0]
        AL, RANK, _ = dn.shape
        C = keys.shape[1]
        N = T * RP
        H = F // RP
        HL = F // HEAD_DIM
        FOLD = max(1, 16 // R)
        f32, b16 = jnp.float32, jnp.bfloat16
        dma = pltpu.SemaphoreType.DMA
        hbm = pl.BlockSpec(memory_space=pltpu.HBM)
        return pl.pallas_call(
            functools.partial(kernel, T, RP, R, F, NB, RANK, AL, C),
            out_shape=jax.ShapeDtypeStruct((R, F), b16),
            in_specs=[hbm] * 8,
            out_specs=pl.BlockSpec(memory_space=pltpu.VMEM),
            scratch_shapes=[
                pltpu.SMEM(lengths.shape, jnp.int32),
                pltpu.SMEM(index.shape, jnp.int32),
                pltpu.VMEM((R, F), b16),
                pltpu.VMEM(keys.shape[1:], b16),
                pltpu.VMEM(values.shape[1:], b16),
                pltpu.VMEM((T, F, H), b16),
                pltpu.VMEM(dn.shape, b16),
                pltpu.VMEM(up.shape, b16),
                pltpu.VMEM((T, HL, HEAD_DIM), f32),
                pltpu.VMEM((T, HL, HEAD_DIM), f32),
                pltpu.VMEM((T, HL, HEAD_DIM), f32),
                pltpu.VMEM((N, HL, HEAD_DIM), f32),
                pltpu.VMEM((T, NB, 128), f32),
                pltpu.VMEM((N, R * FOLD, H // FOLD), b16),
                pltpu.VMEM((N, R * FOLD, H // FOLD), b16),
                pltpu.VMEM((RP, R, F), f32),
                pltpu.VMEM((R, F), f32),
                dma((7,)),
                dma((T,)),
                *[dma((1,)) for _ in range(8)],
                dma((1,)), dma((1,)),
            ],
            compiler_params=pltpu.CompilerParams(
                collective_id=0, has_side_effects=True,
                vmem_limit_bytes=63 * 1024 * 1024,
            ),
        )(query, keys, values, lengths, index, w, dn, up)

    return jax.shard_map(
        local,
        mesh=mesh,
        in_specs=(
            P(("groups", "replica"), "tensor"),
            P(("groups", "replica", "tensor"), None, None),
            P(("groups", "replica", "tensor"), None, None),
            P(("groups", "replica", "tensor")),
            P("groups"),
            P("tensor", None),
            P(("groups", "replica"), None, "tensor"),
            P(("groups", "replica"), None, "tensor"),
        ),
        out_specs=P(("groups", "replica"), "tensor"),
        check_vma=False,
    )
```

```python
import functools

import jax
import jax.numpy as jnp
from jax import lax
from jax.experimental import pallas as pl
from jax.experimental.pallas import tpu as pltpu
from jax.sharding import PartitionSpec as P

KV_HEADS = 8
HEAD_DIM = 128
GROUP = 8
MESH = pl.DeviceIdType.MESH
NT = (((1,), (1,)), ((), ()))
NN = (((1,), (0,)), ((), ()))


def kernel(
    T, RP, R, F, NB, RANK, AL, C,
    q_hbm, k_hbm, v_hbm, len_ref, idx_hbm, w_hbm, dn_hbm, up_hbm, out_ref,
    idx_ref, q_v, k_v, v_v, w_v, dn_v, up_v,
    q_send, q_recv, a_send, a_recv, e_buf, p_send, p_recv, d_buf, d_recv,
    loc_sem, w_sem,
    qs_sem, qr_sem, as_sem, ar_sem, es_sem, er_sem, ps_sem, pr_sem, ds_sem, dr_sem,
):
    t = lax.axis_index("tensor")
    r = lax.axis_index("replica")
    N = T * RP
    me = r * T + t
    H = F // RP
    HL = F // HEAD_DIM
    FOLD = max(1, 16 // R)
    PACK = 256 // RANK

    def wrap(x):
        return jnp.where(x >= T, x - T, x)

    q_cp = pltpu.make_async_copy(q_hbm, q_v, loc_sem.at[0])
    k_cp = pltpu.make_async_copy(k_hbm.at[0], k_v, loc_sem.at[1])
    v_cp = pltpu.make_async_copy(v_hbm.at[0], v_v, loc_sem.at[2])
    dn_cp = pltpu.make_async_copy(dn_hbm, dn_v, loc_sem.at[3])
    up_cp = pltpu.make_async_copy(up_hbm, up_v, loc_sem.at[4])

    def w_cp(tt):
        cols = pl.ds(pl.multiple_of(tt * F + r * H, 128), H)
        return pltpu.make_async_copy(w_hbm.at[:, cols], w_v.at[tt], w_sem.at[tt])

    idx_cp = pltpu.make_async_copy(idx_hbm, idx_ref, loc_sem.at[5])

    def many(buf, count, send, recv):
        part = buf.at[pl.ds(0, count)]
        return pltpu.make_async_remote_copy(
            src_ref=part, dst_ref=part, send_sem=send.at[0], recv_sem=recv.at[0],
            device_id={"replica": 1 - r}, device_id_type=MESH,
        )

    q_all_rc = many(q_recv, T - 1, qs_sem, qr_sem)
    a_all_rc = many(a_recv, N - 1, as_sem, ar_sem)
    e_all_rc = many(e_buf, T - 1, es_sem, er_sem)
    p_all_rc = many(p_recv, N - 1, ps_sem, pr_sem)

    q_cp.start()
    idx_cp.start()
    barrier = pltpu.get_barrier_semaphore()

    def greet(rr, dst):
        pl.semaphore_signal(
            barrier, inc=1, device_id={"tensor": dst, "replica": rr}, device_id_type=MESH
        )

    @pl.loop(1, T)
    def _(i):
        for rr in range(RP):
            greet(rr, wrap(t + i))

    greet(1 - r, t)

    k_cp.start()
    v_cp.start()
    dn_cp.start()

    @pl.loop(1, T + 1)
    def _(i):
        w_cp(wrap(t + i)).start()

    up_cp.start()

    q_cp.wait()
    idx_cp.wait()
    q_all = q_v[...].astype(jnp.float32)
    for h in range(HL):
        q_send[:, h, :] = q_all[:, h * HEAD_DIM:(h + 1) * HEAD_DIM]

    pl.semaphore_wait(barrier, N - 1)

    def q_rc(dst, src):
        return pltpu.make_async_remote_copy(
            src_ref=q_send.at[dst], dst_ref=q_recv.at[src],
            send_sem=qs_sem.at[0], recv_sem=qr_sem.at[0],
            device_id={"tensor": dst}, device_id_type=MESH,
        )

    @pl.loop(1, T)
    def _(i):
        q_rc(wrap(t + i), t).start()

    q_recv[t] = q_send[t]
    k_cp.wait()

    q_all_rc.wait_recv()

    n_per = T // KV_HEADS if T > KV_HEADS else 1
    live = len_ref[0]
    live_mask = lax.broadcasted_iota(jnp.int32, (2 * GROUP, C), 1) < live
    zero = jnp.zeros((GROUP, HEAD_DIM), jnp.float32)

    def heads_of(kv):
        if HL >= GROUP:
            per = HL // GROUP
            rows = q_recv[kv // per]
            return rows[(kv % per) * GROUP:(kv % per + 1) * GROUP]
        return jnp.concatenate([q_recv[kv * n_per + i] for i in range(n_per)], axis=0)

    weights = []
    for p in range(KV_HEADS // 2):
        pair = jnp.concatenate(
            [
                jnp.concatenate([heads_of(2 * p), zero], axis=1),
                jnp.concatenate([zero, heads_of(2 * p + 1)], axis=1),
            ],
            axis=0,
        ).astype(jnp.bfloat16)
        cols = slice(p * 2 * HEAD_DIM, (p + 1) * 2 * HEAD_DIM)
        s = lax.dot_general(pair, k_v[:, cols], NT, preferred_element_type=jnp.float32)
        s = jnp.where(live_mask, s * HEAD_DIM ** (-0.5), -1e30)
        top = jnp.max(s, axis=1, keepdims=True)
        e = jnp.where(live_mask, jnp.exp(s - top), 0.0)
        weights.append((e / jnp.sum(e, axis=1, keepdims=True)).astype(jnp.bfloat16))

    v_cp.wait()
    for p in range(KV_HEADS // 2):
        cols = slice(p * 2 * HEAD_DIM, (p + 1) * 2 * HEAD_DIM)
        o = lax.dot_general(weights[p], v_v[:, cols], NN, preferred_element_type=jnp.float32)
        o = o.astype(jnp.bfloat16).astype(jnp.float32)
        for half in range(2):
            kv = 2 * p + half
            rows = o[half * GROUP:(half + 1) * GROUP, half * HEAD_DIM:(half + 1) * HEAD_DIM]
            if HL >= GROUP:
                per = HL // GROUP
                a_send[kv // per, (kv % per) * GROUP:(kv % per + 1) * GROUP, :] = rows
            else:
                for i in range(n_per):
                    a_send[kv * n_per + i] = rows[i * HL:(i + 1) * HL]

    def a_rc(rr, dst, src):
        return pltpu.make_async_remote_copy(
            src_ref=a_send.at[dst], dst_ref=a_recv.at[src],
            send_sem=as_sem.at[0], recv_sem=ar_sem.at[0],
            device_id={"tensor": dst, "replica": rr}, device_id_type=MESH,
        )

    @pl.loop(1, T)
    def _(i):
        dst = wrap(t + T - i)
        for rr in range(RP):
            a_rc(rr, dst, me).start()

    a_rc(1 - r, t, me).start()

    a_recv[me] = a_send[t]
    dn_cp.wait()

    a_all_rc.wait_recv()

    rows = jnp.concatenate(
        [a_recv[:, h, :] for h in range(HL)], axis=1
    ).astype(jnp.bfloat16)

    ids = [idx_ref[b] - r * AL for b in range(NB)]
    row2 = lax.broadcasted_iota(jnp.int32, (NB, 128), 0)
    here = jnp.zeros((NB, 128), jnp.int32)
    for b in range(NB):
        ok = jnp.where((ids[b] >= 0) & (ids[b] < AL), 1, 0)
        here = jnp.where(row2 == b, ok, here)
    local = [jnp.clip(i, 0, AL - 1) for i in ids]
    rowp = lax.broadcasted_iota(jnp.int32, (NB, 256), 0)
    slot = lax.broadcasted_iota(jnp.int32, (NB, 256), 1) // RANK
    part = jnp.zeros((NB, 256), jnp.float32)
    for j in range(NB // PACK):
        panels = jnp.concatenate([dn_v[local[j * PACK + b]] for b in range(PACK)], axis=0)
        o = lax.dot_general(rows, panels, NT, preferred_element_type=jnp.float32)
        part = jnp.where(rowp == j * PACK + slot, o, part)
    e_buf[t] = jnp.where(here > 0, part[:, :128] + part[:, 128:], 0.0)

    def e_rc(dst, src):
        return pltpu.make_async_remote_copy(
            src_ref=e_buf.at[src], dst_ref=e_buf.at[src],
            send_sem=es_sem.at[0], recv_sem=er_sem.at[0],
            device_id={"tensor": dst}, device_id_type=MESH,
        )

    @pl.loop(1, T)
    def _(i):
        e_rc(wrap(t + i), t).start()

    def p_rc(rr, dst, src):
        return pltpu.make_async_remote_copy(
            src_ref=p_send.at[rr * T + dst], dst_ref=p_recv.at[src],
            send_sem=ps_sem.at[0], recv_sem=pr_sem.at[0],
            device_id={"tensor": dst, "replica": rr}, device_id_type=MESH,
        )

    def project(tt):
        w_cp(tt).wait()
        acc = lax.dot_general(rows, w_v[tt], NN, preferred_element_type=jnp.float32)
        for rr in range(RP):
            block = acc[rr * R:(rr + 1) * R]
            if FOLD > 1:
                wide = H // FOLD
                block = jnp.concatenate(
                    [block[:, f * wide:(f + 1) * wide] for f in range(FOLD)], axis=0
                )
            p_send[rr * T + tt] = block.astype(jnp.bfloat16)

    @pl.loop(1, T)
    def _(i):
        tt = wrap(t + i)
        project(tt)
        for rr in range(RP):
            p_rc(rr, tt, me).start()

    project(t)
    p_rc(1 - r, t, me).start()
    p_recv[me] = p_send[me]

    up_cp.wait()

    e_all_rc.wait_recv()

    total = e_buf[0]
    for i in range(1, T):
        total = total + e_buf[i]
    total = total.astype(jnp.bfloat16).astype(jnp.float32)
    total = jnp.concatenate([total, total], axis=1)
    delta = jnp.zeros((NB, F), jnp.float32)
    for j in range(NB // PACK):
        panels = jnp.concatenate([up_v[local[j * PACK + b]] for b in range(PACK)], axis=0)
        lhs = jnp.where(rowp == j * PACK + slot, total, 0.0).astype(jnp.bfloat16)
        delta = delta + lax.dot_general(lhs, panels, NN, preferred_element_type=jnp.float32)
    for rr in range(RP):
        d_buf[rr] = delta[rr * R:(rr + 1) * R]
    d_rc = pltpu.make_async_remote_copy(
        src_ref=d_buf.at[1 - r], dst_ref=d_recv,
        send_sem=ds_sem.at[0], recv_sem=dr_sem.at[0],
        device_id={"replica": 1 - r}, device_id_type=MESH,
    )
    d_rc.start()

    q_all_rc.wait_send()
    e_all_rc.wait_send()
    a_all_rc.wait_send()

    p_all_rc.wait_recv()

    d_rc.wait_recv()
    for rr in range(RP):
        base = p_recv[rr * T].astype(jnp.float32)
        for i in range(1, T):
            base = base + p_recv[rr * T + i].astype(jnp.float32)
        if FOLD > 1:
            base = jnp.concatenate([base[f * R:(f + 1) * R] for f in range(FOLD)], axis=1)
        cols = slice(rr * H, (rr + 1) * H)
        add = d_buf[r, :, cols] + d_recv[:, cols]
        out_ref[:, cols] = (base + add).astype(jnp.bfloat16)

    p_all_rc.wait_send()

    d_rc.wait_send()


def solution(mesh):
    T = mesh.shape["tensor"]
    RP = mesh.shape["replica"]

    def local(query, keys, values, lengths, index, w, dn, up):
        R, F = query.shape
        NB = index.shape[0]
        AL, RANK, _ = dn.shape
        C = keys.shape[1]
        N = T * RP
        H = F // RP
        HL = F // HEAD_DIM
        FOLD = max(1, 16 // R)
        f32, b16 = jnp.float32, jnp.bfloat16
        dma = pltpu.SemaphoreType.DMA
        smem = pl.BlockSpec(memory_space=pltpu.SMEM)
        hbm = pl.BlockSpec(memory_space=pltpu.HBM)
        return pl.pallas_call(
            functools.partial(kernel, T, RP, R, F, NB, RANK, AL, C),
            out_shape=pltpu.VMEM((R, F), b16),
            in_specs=[hbm] * 3 + [smem] + [hbm] * 4,
            out_specs=pl.BlockSpec(memory_space=pltpu.VMEM),
            scratch_shapes=[
                pltpu.SMEM(index.shape, jnp.int32),
                pltpu.VMEM((R, F), b16),
                pltpu.VMEM(keys.shape[1:], b16),
                pltpu.VMEM(values.shape[1:], b16),
                pltpu.VMEM((T, F, H), b16),
                pltpu.VMEM(dn.shape, b16),
                pltpu.VMEM(up.shape, b16),
                pltpu.VMEM((T, HL, HEAD_DIM), f32),
                pltpu.VMEM((T, HL, HEAD_DIM), f32),
                pltpu.VMEM((T, HL, HEAD_DIM), f32),
                pltpu.VMEM((N, HL, HEAD_DIM), f32),
                pltpu.VMEM((T, NB, 128), f32),
                pltpu.VMEM((N, R * FOLD, H // FOLD), b16),
                pltpu.VMEM((N, R * FOLD, H // FOLD), b16),
                pltpu.VMEM((RP, R, F), f32),
                pltpu.VMEM((R, F), f32),
                dma((6,)),
                dma((T,)),
                *[dma((1,)) for _ in range(8)],
                dma((1,)), dma((1,)),
            ],
            compiler_params=pltpu.CompilerParams(
                collective_id=0, has_side_effects=True,
                vmem_limit_bytes=63 * 1024 * 1024,
            ),
        )(query, keys, values, lengths, index, w, dn, up)

    return jax.shard_map(
        local,
        mesh=mesh,
        in_specs=(
            P(("groups", "replica"), "tensor"),
            P(("groups", "replica", "tensor"), None, None),
            P(("groups", "replica", "tensor"), None, None),
            P(("groups", "replica", "tensor")),
            P("groups"),
            P("tensor", None),
            P(("groups", "replica"), None, "tensor"),
            P(("groups", "replica"), None, "tensor"),
        ),
        out_specs=P(("groups", "replica"), "tensor"),
        check_vma=False,
    )
```
